32 devices in a mesh: grp: 2 (over x), row: 8 (over z, y), lag: 2 (over core).
Axes of the slice: x: 2, y: 2, z: 4, core: 2. Of those that a mesh axis runs over, the one named last changes fastest.
Arguments:
- history: bfloat16 [400, 2080], P('grp', 'lag'), parts along dimension 0, may hold values from -6 to 6
- kernel: bfloat16 [256, 200, 2048], P(('grp', 'row'), None, 'lag'), parts along dimension 0, may hold values from -0.009765625 to 0.009765625
- tile_rows: int32 [128, 16], P(('grp', 'row')), parts along dimension 0, may hold values from 0 to 15
- tile_counts: int32 [128], P(('grp', 'row')), parts along dimension 0, may hold values from 1 to 16
- owner: int32 [128, 1], P(('grp', 'row')), parts along dimension 0, may hold values from 0 to 7; in each aligned block of 8 rows (0 to 7, 8 to 15, ...) at most 2 rows name the same one
- spline: bfloat16 [128, 16, 128], P(('grp', 'row')), parts along dimension 0, may hold values from -0.5 to 0.5
- mode_shapes: float32 [2048, 200], P(('grp', 'row')), parts along dimension 0, may hold values from -0.1875 to 0.1875
Outputs:
- nodal_forces: float32 [32, 2048], P('lag', ('grp', 'row')), parts along dimension 1
- modal_forces: float32 [32, 400], P('lag', 'grp'), parts along dimension 1
The draws below stay inside these ranges and needn't reach their ends.
There are 2 independent parts, one for each index of `grp`. The reference program is written for one: setup_inputs(seed, part) draws one part's arguments, and reference() takes and returns one part's arrays. A program takes and returns all parts, laid end to end along the dimension named above; each array names one. Nothing has to cross between parts.
Inputs may be any that keep to these rules, and one draw needn't show every extreme that they name: Among the tiles of one device at most 2 have the same owner, and some owner has exactly 2.
All inputs are finite; a program needn't handle non-finite values.
Results may differ from the reference program's by a relative error of at most 0.003.
Values may be sent and summed in bfloat16 or wider, within the bound.
A program may use at most 64 MiB of HBM per device.

```python
import math
import jax
import jax.numpy as jnp
import numpy as np
from jax import lax

MODES = 200
LAGS = 2048
TSTEP = 32
PR_DEV = 16
TP = 16
NDOF_DEV = 128
CAP = 2
TILES_DEV = 8
TILES = 64
PRESS = 128
NDOF = 1024
HLEN = 2080
N_ROW = 8


def plant(entries, key, smallest, top_value):
    index_at = [jax.random.randint(jax.random.fold_in(key, axis), (), 0, length) for axis, length in enumerate(entries.shape)]
    longest = entries.shape.index(max(entries.shape))
    beside = index_at[:longest] + [(index_at[longest] + 1) % entries.shape[longest]] + index_at[longest + 1:]
    return entries.at[tuple(index_at)].set(smallest).at[tuple(beside)].set(top_value)


def steps_of(key, dims, split, least, high):
    level, own = 1.0, jax.random.fold_in(key, 6)
    for dim, shards_of in split:
        steps = jnp.exp(jax.random.uniform(jax.random.fold_in(own, dim), (shards_of,), jnp.float32, least / len(split), high / len(split)))
        level = level * jnp.repeat(steps, dims[dim] // shards_of).reshape([-1 if axis == dim else 1 for axis in range(len(dims))])
    return level


def assign_block(stream_key, own, number, rows, number_of, top, most, slope):
    ranking = jax.random.permutation(stream_key, number_of)
    packed, common = load_shares(number_of, rows * top, most, slope, True), load_shares(number_of, rows * top, most, slope, False)
    places = jnp.arange(number_of)

    def named(tallies, offset_by):
        used = int((tallies > 0).sum())
        fixed = max(1, used // 4)
        shifted = fixed + (places - fixed + offset_by * (used - fixed)) % max(1, number_of - fixed)
        return jnp.zeros((number_of,), jnp.int32).at[ranking[jnp.where(places < fixed, places, shifted)]].set(jnp.asarray(tallies, jnp.int32))

    tallies = jnp.where(number % 4 == 0, named(packed, number // 4), named(common, number - number // 4 - 1))
    mixed = jax.random.permutation(jax.random.fold_in(own, 3), number_of)
    giver, receiver = mixed[0:number_of // 2 * 2:2], mixed[1:number_of // 2 * 2:2]
    room = jnp.minimum(tallies[giver] - 1, most - tallies[receiver]) // 2
    room = jnp.where((giver == ranking[0]) | (receiver == ranking[0]) | (tallies[receiver] == 0), 0, jnp.maximum(room, 0))
    shifted = jax.random.randint(jax.random.fold_in(own, 4), (number_of // 2,), 0, 1 << 20) % (room + 1)
    tallies = tallies.at[giver].add(-shifted).at[receiver].add(shifted)
    members = jnp.searchsorted(jnp.cumsum(tallies), jnp.arange(rows * top), side="right").astype(jnp.int32)
    grid = members.reshape(top, rows).T
    grid = grid[jax.random.permutation(jax.random.fold_in(own, 1), rows)]
    offset_by = jax.random.randint(jax.random.fold_in(own, 2), (rows, 1), 0, top)
    return jnp.take_along_axis(grid, (jnp.arange(top)[None, :] + offset_by) % top, axis=1)


def load_shares(count, total, limit, skew, full):
    loads = [(1 << 20) // math.isqrt(grade ** skew) + 1 for grade in range(1, count + 1)]
    largest = limit if full else min(limit, max(-(-total // count), total * loads[0] // sum(loads)))
    least = 1 if total - largest >= count - 1 else 0
    given, surplus = [largest] + [least] * (count - 1), total - largest - least * (count - 1)
    while surplus > 0:
        candidates = [i for i in range(1, count) if given[i] < largest] or [i for i in range(1, count) if given[i] < limit]
        pool, budget = sum([loads[i] for i in candidates]), surplus
        for i in candidates:
            addition = min(limit - given[i], max(1, budget * loads[i] // pool), surplus)
            given[i] = given[i] + addition
            surplus = surplus - addition
    return np.array(given)


def gaussian(stream_key, extent, width, limit, pieces=(), kind=jnp.bfloat16):
    drawn = jax.random.normal(stream_key, extent, jnp.float32) * width
    if len(pieces) > 0:
        drawn = steps_of(stream_key, extent, pieces, -0.22, 0.18) * drawn
    return jnp.clip(drawn, min=-limit, max=limit).astype(kind)


def setup_inputs(seed: int = 0, part: int = 0) -> dict:
    splits = jax.random.split(jax.random.key(seed), 8)
    part_splits = jax.random.split(jax.random.fold_in(splits[7], part), 8)
    history = gaussian(part_splits[0], (MODES, HLEN), 1.0, 6.0, ((1, 2),))
    kernel = gaussian(part_splits[1], (PRESS, MODES, LAGS), (MODES * LAGS) ** -0.5, 0.009765625, ((0, 8), (2, 2)))
    tile_rows = plant(jax.random.randint(part_splits[2], (TILES, TP), 0, PR_DEV), jax.random.fold_in(part_splits[2], 1), 0, PR_DEV - 1).astype(jnp.int32)
    tile_counts = plant(jax.random.randint(part_splits[3], (TILES,), 1, TP + 1), jax.random.fold_in(part_splits[3], 1), 1, TP).astype(jnp.int32)
    owner_keys = jax.random.split(jax.random.fold_in(part_splits[4], 1), TILES // TILES_DEV)
    owner_turns = jax.random.permutation(jax.random.fold_in(part_splits[4], 3), TILES // TILES_DEV)
    owner = jax.vmap(lambda own, number: assign_block(jax.random.fold_in(part_splits[4], 2), own, number, TILES_DEV, N_ROW, 1, CAP, 2))(owner_keys, owner_turns).reshape((TILES, 1))
    spline = gaussian(part_splits[5], (TILES, TP, NDOF_DEV), (TP * CAP * 4) ** -0.5, 0.5, ((0, 8),))
    mode_shapes = gaussian(part_splits[6], (NDOF, MODES), NDOF ** -0.5, 0.1875, ((0, 8),), jnp.float32)
    return dict(history=history, kernel=kernel, tile_rows=tile_rows, tile_counts=tile_counts, owner=owner, spline=spline, mode_shapes=mode_shapes)


def reference(history, kernel, tile_rows, tile_counts, owner, spline, mode_shapes):
    reversed_hist = history[:, ::-1]
    window = reversed_hist[:, 1:LAGS + TSTEP][None]
    conv = lax.conv_general_dilated(window, kernel, (1,), "VALID", dimension_numbers=("NCH", "OIH", "NCH"), preferred_element_type=jnp.float32)
    pressure = conv[0].T[::-1]
    pressure = pressure.astype(jnp.bfloat16)
    base_rows = (jnp.arange(TILES, dtype=jnp.int32) // TILES_DEV) * PR_DEV
    global_rows = tile_rows + base_rows[:, None]
    tile_in = pressure[:, global_rows]
    valid = jnp.arange(TP, dtype=jnp.int32)[None, :] < tile_counts[:, None]
    tile_in = jnp.where(valid[None, :, :], tile_in, jnp.zeros_like(tile_in))
    tile_out = jnp.einsum("tip,ipn->itn", tile_in.astype(jnp.float32), spline.astype(jnp.float32))
    onehot = (owner[:, 0][:, None] == jnp.arange(N_ROW, dtype=jnp.int32)[None, :]).astype(jnp.float32)
    nodal = jnp.einsum("itn,id->tdn", tile_out, onehot, precision=lax.Precision.HIGHEST)
    nodal = nodal.reshape(TSTEP, NDOF)
    modal = jnp.dot(nodal, mode_shapes, precision=lax.Precision.HIGHEST)
    return nodal, modal
```

```python
import functools

import jax
import jax.numpy as jnp
from jax import lax
from jax.experimental import pallas as pl
from jax.experimental.pallas import tpu as pltpu
from jax.sharding import PartitionSpec as P

TSTEP = 32
BLOCK = 128
MESH_ID = pl.DeviceIdType.MESH
F32 = jnp.float32
BF16 = jnp.bfloat16


def body(
    rows,
    hist_hbm,
    kern_hbm,
    trow_hbm,
    tcnt_hbm,
    own_hbm,
    spl_hbm,
    mode_hbm,
    nodal_out,
    modal_out,
    hist_in,
    kern,
    trow,
    tcnt,
    own,
    spl,
    mode,
    hist_t,
    window,
    part,
    part_in,
    force,
    force_send,
    force_in,
    modal_send,
    modal_in,
    local_sem,
    kern_sem,
    hist_sem,
    part_sem,
    force_ssem,
    force_rsem,
    modal_ssem,
    modal_rsem,
):
    lag = lax.axis_index("lag")
    me = lax.axis_index("row")
    press = kern.shape[0]
    pairs = press // 2
    lags = kern.shape[2]
    blocks = lags // BLOCK
    hlen = hist_in.shape[1]
    half = TSTEP // 2

    hist_copy = pltpu.make_async_copy(hist_hbm, hist_in, local_sem.at[0])
    hist_copy.start()
    barrier = pltpu.get_barrier_semaphore()
    pl.semaphore_signal(barrier, inc=1, device_id={"lag": 1 - lag}, device_id_type=MESH_ID)
    for o in range(1, rows):
        pl.semaphore_signal(
            barrier, inc=1, device_id={"row": lax.rem(me + o, rows)}, device_id_type=MESH_ID
        )
    small = [
        pltpu.make_async_copy(src, dst, local_sem.at[1 + n])
        for n, (src, dst) in enumerate(
            [(trow_hbm, trow), (tcnt_hbm, tcnt), (own_hbm, own), (spl_hbm, spl), (mode_hbm, mode)]
        )
    ]

    def kern_copy(p):
        at = pl.ds(2 * p, 2)
        return pltpu.make_async_copy(kern_hbm.at[at], kern.at[at], kern_sem.at[p])

    for p in range(pairs):
        kern_copy(p).start()
    for copy in small:
        copy.start()

    hist_copy.wait()
    hist_t[...] = hist_in[...].T
    pl.semaphore_wait(barrier, rows)
    hist_send = pltpu.make_async_remote_copy(
        src_ref=hist_t,
        dst_ref=window.at[pl.ds(pl.multiple_of(half * lag, half), hlen)],
        send_sem=hist_sem.at[0],
        recv_sem=hist_sem.at[1],
        device_id={"lag": 1 - lag},
        device_id_type=MESH_ID,
    )
    hist_send.start()
    window[pl.ds(pl.multiple_of(hlen * lag, half), half), :] = hist_t[
        pl.ds(pl.multiple_of((hlen - half) * (1 - lag), half), half), :
    ]

    for copy in small:
        copy.wait()
    tiles, tp = trow.shape
    picks = tiles * tp
    e_lane = lax.broadcasted_iota(jnp.int32, (tp, picks), 1)
    e_row = lax.broadcasted_iota(jnp.int32, (tp, picks), 0)
    spread = (lax.rem(e_lane, tp) == e_row).astype(BF16)
    t_lane = lax.broadcasted_iota(jnp.int32, (tiles, picks), 1)
    t_row = lax.broadcasted_iota(jnp.int32, (tiles, picks), 0)
    mine = lax.div(t_lane, tp) == t_row
    row_at = jnp.dot(trow[...].astype(F32).astype(BF16), spread, preferred_element_type=F32)
    row_at = jnp.sum(jnp.where(mine, row_at, 0.0), axis=0, keepdims=True)
    own_at = jnp.sum(jnp.where(mine, own[...].astype(F32), 0.0), axis=0, keepdims=True)
    lane = lax.broadcasted_iota(jnp.int32, (1, picks), 1)
    tile_at = lax.div(lane, tp)
    count_at = jnp.zeros((1, picks), jnp.int32)
    for i in range(tiles):
        count_at = jnp.where(tile_at == i, tcnt[i], count_at)
    row_at = jnp.where(lax.rem(lane, tp) < count_at, row_at, -1.0)
    r_iota = lax.broadcasted_iota(jnp.int32, (BLOCK, picks), 0).astype(F32)
    picker = (r_iota == row_at).astype(F32).astype(BF16)

    hist_send.wait()

    b_lane = lax.broadcasted_iota(jnp.int32, (1, 2 * BLOCK), 1)
    shift = (BLOCK - 1) - lax.rem(b_lane, BLOCK)
    lane1 = lax.broadcasted_iota(jnp.int32, (TSTEP, BLOCK), 1)

    def pair(p, acc):
        kern_copy(p).wait()
        total = None
        for a in range(blocks):
            cols = slice(a * BLOCK, (a + 1) * BLOCK)
            w = jnp.concatenate([kern[2 * p, :, cols], kern[2 * p + 1, :, cols]], axis=1)
            start = lags - BLOCK * (a + 1)
            x = window[start : start + BLOCK + TSTEP, :]
            y = jnp.dot(x, w, preferred_element_type=F32)
            total = y if total is None else total + y
        bit, length = BLOCK // 2, BLOCK
        while bit >= 8:
            length = TSTEP + bit
            up = total[bit : bit + length]
            total = jnp.where((shift & bit) != 0, up, total[:length])
            bit //= 2
        for bit in (4, 2, 1):
            up = pltpu.roll(total, total.shape[0] - bit, 0)
            total = jnp.where((shift & bit) != 0, up, total)
        total = total[:TSTEP]
        s0 = jnp.sum(total[:, :BLOCK], axis=1, keepdims=True)
        s1 = jnp.sum(total[:, BLOCK:], axis=1, keepdims=True)
        acc = jnp.where(lane1 == 2 * p, s0, acc)
        return jnp.where(lane1 == 2 * p + 1, s1, acc)

    acc = lax.fori_loop(0, pairs, pair, jnp.zeros((TSTEP, BLOCK), F32))
    part[...] = acc.reshape(2, half, BLOCK)
    part_send = pltpu.make_async_remote_copy(
        src_ref=part.at[1 - lag],
        dst_ref=part_in,
        send_sem=part_sem.at[0],
        recv_sem=part_sem.at[1],
        device_id={"lag": 1 - lag},
        device_id_type=MESH_ID,
    )
    part_send.start()
    part_send.wait_recv()
    pressure = (part[lag] + part_in[...]).astype(BF16)

    tile_in = jnp.dot(pressure, picker, preferred_element_type=F32)
    owned = jnp.concatenate(
        [jnp.where(own_at == float(d), tile_in, 0.0) for d in range(rows)], axis=0
    ).astype(BF16)
    flat = jnp.dot(owned, spl[...].reshape(picks, spl.shape[2]), preferred_element_type=F32)
    force[...] = flat.reshape(rows, half, spl.shape[2])
    force_send[...] = force[...].astype(force_send.dtype)

    def exchange(sources, dest, ssem, rsem):
        copies = [
            pltpu.make_async_remote_copy(
                src_ref=sources(lax.rem(me + o, rows)),
                dst_ref=dest.at[o - 1],
                send_sem=ssem.at[o - 1],
                recv_sem=rsem.at[o - 1],
                device_id={"row": lax.rem(me + o, rows)},
                device_id_type=MESH_ID,
            )
            for o in range(1, rows)
        ]
        for copy in copies:
            copy.start()
        return copies

    force_copies = exchange(lambda d: force_send.at[d], force_in, force_ssem, force_rsem)
    nodal = force[me]
    for o, copy in enumerate(force_copies):
        copy.wait_recv()
        nodal = nodal + force_in[o].astype(F32)
    share = jnp.dot(
        nodal, mode[...], preferred_element_type=F32, precision=lax.Precision.HIGHEST
    )
    modal_send[...] = share.astype(modal_send.dtype)
    modal_copies = exchange(lambda d: modal_send, modal_in, modal_ssem, modal_rsem)
    nodal_out[...] = nodal
    for o, copy in enumerate(modal_copies):
        copy.wait_recv()
        share = share + modal_in[o].astype(F32)
    modal_out[...] = share
    part_send.wait_send()
    for copy in force_copies + modal_copies:
        copy.wait_send()


def on_device(history, kernel, tile_rows, tile_counts, owner, spline, mode_shapes):
    rows = lax.axis_size("row")
    modes, hlen = history.shape
    press, _, lags = kernel.shape
    tiles, tp = tile_rows.shape
    ndof = spline.shape[2]
    half = TSTEP // 2
    dma = pltpu.SemaphoreType.DMA
    return pl.pallas_call(
        functools.partial(body, rows),
        out_shape=(
            jax.ShapeDtypeStruct((half, ndof), F32),
            jax.ShapeDtypeStruct((half, modes), F32),
        ),
        in_specs=[pl.BlockSpec(memory_space=pl.ANY)] * 7,
        out_specs=(
            pl.BlockSpec(memory_space=pltpu.VMEM),
            pl.BlockSpec(memory_space=pltpu.VMEM),
        ),
        scratch_shapes=[
            pltpu.VMEM((modes, hlen), BF16),
            pltpu.VMEM((press, modes, lags), BF16),
            pltpu.VMEM((tiles, tp), jnp.int32),
            pltpu.SMEM((tiles,), jnp.int32),
            pltpu.VMEM((tiles, 1), jnp.int32),
            pltpu.VMEM(spline.shape, BF16),
            pltpu.VMEM(mode_shapes.shape, F32),
            pltpu.VMEM((hlen, modes), BF16),
            pltpu.VMEM((hlen + half, modes), BF16),
            pltpu.VMEM((2, half, BLOCK), F32),
            pltpu.VMEM((half, BLOCK), F32),
            pltpu.VMEM((rows, half, ndof), F32),
            pltpu.VMEM((rows, half, ndof), BF16),
            pltpu.VMEM((rows - 1, half, ndof), BF16),
            pltpu.VMEM((half, modes), BF16),
            pltpu.VMEM((rows - 1, half, modes), BF16),
            dma((6,)),
            dma((press // 2,)),
            dma((2,)),
            dma((2,)),
            dma((rows - 1,)),
            dma((rows - 1,)),
            dma((rows - 1,)),
            dma((rows - 1,)),
        ],
        compiler_params=pltpu.CompilerParams(
            collective_id=0, has_side_effects=True, vmem_limit_bytes=40 * 1024 * 1024
        ),
    )(history, kernel, tile_rows, tile_counts, owner, spline, mode_shapes)


def solution(mesh):
    return jax.shard_map(
        on_device,
        mesh=mesh,
        in_specs=(
            P("grp", "lag"),
            P(("grp", "row"), None, "lag"),
            P(("grp", "row"), None),
            P(("grp", "row")),
            P(("grp", "row"), None),
            P(("grp", "row"), None, None),
            P(("grp", "row"), None),
        ),
        out_specs=(P("lag", ("grp", "row")), P("lag", "grp")),
        check_vma=False,
    )
```

```python
import functools

import jax
import jax.numpy as jnp
from jax import lax
from jax.experimental import pallas as pl
from jax.experimental.pallas import tpu as pltpu
from jax.sharding import PartitionSpec as P

TSTEP = 32
BLOCK = 128
MESH_ID = pl.DeviceIdType.MESH
F32 = jnp.float32
BF16 = jnp.bfloat16


def body(
    rows,
    hist_hbm,
    kern_hbm,
    trow_hbm,
    tcnt_hbm,
    own_hbm,
    spl_hbm,
    mode_hbm,
    nodal_out,
    modal_out,
    hist_in,
    kern,
    trow,
    tcnt,
    own,
    spl,
    mode,
    hist_t,
    window,
    part,
    part_in,
    force,
    force_in,
    modal_send,
    modal_in,
    local_sem,
    kern_sem,
    hist_sem,
    part_sem,
    force_ssem,
    force_rsem,
    modal_ssem,
    modal_rsem,
):
    lag = lax.axis_index("lag")
    me = lax.axis_index("row")
    press = kern.shape[0]
    pairs = press // 2
    lags = kern.shape[2]
    blocks = lags // BLOCK
    hlen = hist_in.shape[1]
    half = TSTEP // 2

    hist_copy = pltpu.make_async_copy(hist_hbm, hist_in, local_sem.at[0])
    hist_copy.start()
    barrier = pltpu.get_barrier_semaphore()
    pl.semaphore_signal(barrier, inc=1, device_id={"lag": 1 - lag}, device_id_type=MESH_ID)
    for o in range(1, rows):
        pl.semaphore_signal(
            barrier, inc=1, device_id={"row": lax.rem(me + o, rows)}, device_id_type=MESH_ID
        )
    small = [
        pltpu.make_async_copy(src, dst, local_sem.at[1 + n])
        for n, (src, dst) in enumerate(
            [(trow_hbm, trow), (tcnt_hbm, tcnt), (own_hbm, own), (spl_hbm, spl), (mode_hbm, mode)]
        )
    ]

    def kern_copy(p):
        at = pl.ds(2 * p, 2)
        return pltpu.make_async_copy(kern_hbm.at[at], kern.at[at], kern_sem.at[p])

    for p in range(pairs):
        kern_copy(p).start()
    for copy in small:
        copy.start()

    hist_copy.wait()
    hist_t[...] = hist_in[...].T
    pl.semaphore_wait(barrier, rows)
    hist_send = pltpu.make_async_remote_copy(
        src_ref=hist_t,
        dst_ref=window.at[pl.ds(pl.multiple_of(half * lag, half), hlen)],
        send_sem=hist_sem.at[0],
        recv_sem=hist_sem.at[1],
        device_id={"lag": 1 - lag},
        device_id_type=MESH_ID,
    )
    hist_send.start()
    window[pl.ds(pl.multiple_of(hlen * lag, half), half), :] = hist_t[
        pl.ds(pl.multiple_of((hlen - half) * (1 - lag), half), half), :
    ]

    for copy in small:
        copy.wait()
    tiles, tp = trow.shape
    picks = tiles * tp
    e_lane = lax.broadcasted_iota(jnp.int32, (tp, picks), 1)
    e_row = lax.broadcasted_iota(jnp.int32, (tp, picks), 0)
    spread = (lax.rem(e_lane, tp) == e_row).astype(BF16)
    t_lane = lax.broadcasted_iota(jnp.int32, (tiles, picks), 1)
    t_row = lax.broadcasted_iota(jnp.int32, (tiles, picks), 0)
    mine = lax.div(t_lane, tp) == t_row
    row_at = jnp.dot(trow[...].astype(F32).astype(BF16), spread, preferred_element_type=F32)
    row_at = jnp.sum(jnp.where(mine, row_at, 0.0), axis=0, keepdims=True)
    lane = lax.broadcasted_iota(jnp.int32, (1, picks), 1)
    tile_at = lax.div(lane, tp)
    count_at = jnp.zeros((1, picks), jnp.int32)
    own_at = jnp.zeros((1, picks), jnp.int32)
    for i in range(tiles):
        count_at = jnp.where(tile_at == i, tcnt[i], count_at)
        own_at = jnp.where(tile_at == i, own[i], own_at)
    row_at = jnp.where(lax.rem(lane, tp) < count_at, row_at, -1.0)
    r_iota = lax.broadcasted_iota(jnp.int32, (BLOCK, picks), 0).astype(F32)
    picker = (r_iota == row_at).astype(F32).astype(BF16)

    hist_send.wait()

    b_lane = lax.broadcasted_iota(jnp.int32, (1, 2 * BLOCK), 1)
    shift = (BLOCK - 1) - lax.rem(b_lane, BLOCK)
    lane1 = lax.broadcasted_iota(jnp.int32, (TSTEP, BLOCK), 1)

    def pair(p, acc):
        kern_copy(p).wait()
        total = None
        for a in range(blocks):
            cols = slice(a * BLOCK, (a + 1) * BLOCK)
            w = jnp.concatenate([kern[2 * p, :, cols], kern[2 * p + 1, :, cols]], axis=1)
            start = lags - BLOCK * (a + 1)
            x = window[start : start + BLOCK + TSTEP, :]
            y = jnp.dot(x, w, preferred_element_type=F32)
            total = y if total is None else total + y
        bit, length = BLOCK // 2, BLOCK
        while bit >= 8:
            length = TSTEP + bit
            up = total[bit : bit + length]
            total = jnp.where((shift & bit) != 0, up, total[:length])
            bit //= 2
        for bit in (4, 2, 1):
            up = pltpu.roll(total, total.shape[0] - bit, 0)
            total = jnp.where((shift & bit) != 0, up, total)
        total = total[:TSTEP]
        s0 = jnp.sum(total[:, :BLOCK], axis=1, keepdims=True)
        s1 = jnp.sum(total[:, BLOCK:], axis=1, keepdims=True)
        acc = jnp.where(lane1 == 2 * p, s0, acc)
        return jnp.where(lane1 == 2 * p + 1, s1, acc)

    acc = lax.fori_loop(0, pairs, pair, jnp.zeros((TSTEP, BLOCK), F32))
    part[...] = acc.reshape(2, half, BLOCK)
    part_send = pltpu.make_async_remote_copy(
        src_ref=part.at[1 - lag],
        dst_ref=part_in,
        send_sem=part_sem.at[0],
        recv_sem=part_sem.at[1],
        device_id={"lag": 1 - lag},
        device_id_type=MESH_ID,
    )
    part_send.start()
    part_send.wait_recv()
    pressure = (part[lag] + part_in[...]).astype(BF16)

    tile_in = jnp.dot(pressure, picker, preferred_element_type=F32)
    owned = jnp.concatenate(
        [jnp.where(own_at == d, tile_in, 0.0) for d in range(rows)], axis=0
    ).astype(BF16)
    flat = jnp.dot(owned, spl[...].reshape(picks, spl.shape[2]), preferred_element_type=F32)
    force[...] = flat.reshape(rows, half, spl.shape[2])

    def exchange(sources, dest, ssem, rsem):
        copies = [
            pltpu.make_async_remote_copy(
                src_ref=sources(lax.rem(me + o, rows)),
                dst_ref=dest.at[o - 1],
                send_sem=ssem.at[o - 1],
                recv_sem=rsem.at[o - 1],
                device_id={"row": lax.rem(me + o, rows)},
                device_id_type=MESH_ID,
            )
            for o in range(1, rows)
        ]
        for copy in copies:
            copy.start()
        return copies

    force_copies = exchange(lambda d: force.at[d], force_in, force_ssem, force_rsem)
    nodal = force[me]
    for o, copy in enumerate(force_copies):
        copy.wait_recv()
        nodal = nodal + force_in[o].astype(F32)
    share = lax.dot_general(
        nodal,
        mode[...],
        (((1,), (1,)), ((), ())),
        preferred_element_type=F32,
        precision=lax.Precision.HIGHEST,
    )
    modal_send[...] = share.astype(modal_send.dtype)
    modal_copies = exchange(lambda d: modal_send, modal_in, modal_ssem, modal_rsem)
    nodal_out[...] = nodal
    for o, copy in enumerate(modal_copies):
        copy.wait_recv()
        share = share + modal_in[o].astype(F32)
    modal_out[...] = share
    part_send.wait_send()
    for copy in force_copies + modal_copies:
        copy.wait_send()


def on_device(history, kernel, tile_rows, tile_counts, owner, spline, mode_shapes):
    rows = lax.axis_size("row")
    modes, hlen = history.shape
    press, _, lags = kernel.shape
    tiles, tp = tile_rows.shape
    ndof = spline.shape[2]
    half = TSTEP // 2
    dma = pltpu.SemaphoreType.DMA
    return pl.pallas_call(
        functools.partial(body, rows),
        out_shape=(
            jax.ShapeDtypeStruct((half, ndof), F32),
            jax.ShapeDtypeStruct((half, modes), F32),
        ),
        in_specs=[pl.BlockSpec(memory_space=pl.ANY)] * 7,
        out_specs=(
            pl.BlockSpec(memory_space=pltpu.VMEM),
            pl.BlockSpec(memory_space=pltpu.VMEM),
        ),
        scratch_shapes=[
            pltpu.VMEM((modes, hlen), BF16),
            pltpu.VMEM((press, modes, lags), BF16),
            pltpu.VMEM((tiles, tp), jnp.int32),
            pltpu.SMEM((tiles,), jnp.int32),
            pltpu.SMEM((tiles,), jnp.int32),
            pltpu.VMEM(spline.shape, BF16),
            pltpu.VMEM((modes, ndof), F32),
            pltpu.VMEM((hlen, modes), BF16),
            pltpu.VMEM((hlen + half, modes), BF16),
            pltpu.VMEM((2, half, BLOCK), F32),
            pltpu.VMEM((half, BLOCK), F32),
            pltpu.VMEM((rows, half, ndof), F32),
            pltpu.VMEM((rows - 1, half, ndof), F32),
            pltpu.VMEM((half, modes), BF16),
            pltpu.VMEM((rows - 1, half, modes), BF16),
            dma((6,)),
            dma((press // 2,)),
            dma((2,)),
            dma((2,)),
            dma((rows - 1,)),
            dma((rows - 1,)),
            dma((rows - 1,)),
            dma((rows - 1,)),
        ],
        compiler_params=pltpu.CompilerParams(
            collective_id=0, has_side_effects=True, vmem_limit_bytes=60 * 1024 * 1024
        ),
    )(history, kernel, tile_rows, tile_counts, owner.reshape(tiles), spline, mode_shapes.T)


def solution(mesh):
    return jax.shard_map(
        on_device,
        mesh=mesh,
        in_specs=(
            P("grp", "lag"),
            P(("grp", "row"), None, "lag"),
            P(("grp", "row"), None),
            P(("grp", "row")),
            P(("grp", "row"), None),
            P(("grp", "row"), None, None),
            P(("grp", "row"), None),
        ),
        out_specs=(P("lag", ("grp", "row")), P("lag", "grp")),
        check_vma=False,
    )
```

```python
import functools

import jax
import jax.numpy as jnp
from jax import lax
from jax.experimental import pallas as pl
from jax.experimental.pallas import tpu as pltpu
from jax.sharding import PartitionSpec as P

TSTEP = 32
BLOCK = 128
MESH_ID = pl.DeviceIdType.MESH
F32 = jnp.float32
BF16 = jnp.bfloat16


def body(
    rows,
    hist_hbm,
    kern_hbm,
    trow_hbm,
    tcnt_hbm,
    own_hbm,
    spl_hbm,
    mode_hbm,
    nodal_out,
    modal_out,
    hist_in,
    kern,
    trow,
    tcnt,
    own,
    spl,
    mode,
    mode_split,
    hist_t,
    window,
    part,
    part_in,
    force,
    force_in,
    modal_send,
    modal_in,
    local_sem,
    kern_sem,
    hist_sem,
    part_sem,
    force_ssem,
    force_rsem,
    modal_ssem,
    modal_rsem,
):
    lag = lax.axis_index("lag")
    me = lax.axis_index("row")
    press = kern.shape[0]
    pairs = press // 2
    lags = kern.shape[2]
    blocks = lags // BLOCK
    hlen = hist_in.shape[1]
    half = TSTEP // 2

    hist_copy = pltpu.make_async_copy(hist_hbm, hist_in, local_sem.at[0])
    hist_copy.start()
    barrier = pltpu.get_barrier_semaphore()
    pl.semaphore_signal(barrier, inc=1, device_id={"lag": 1 - lag}, device_id_type=MESH_ID)
    for o in range(1, rows):
        pl.semaphore_signal(
            barrier, inc=1, device_id={"row": lax.rem(me + o, rows)}, device_id_type=MESH_ID
        )
    small = [
        pltpu.make_async_copy(src, dst, local_sem.at[1 + n])
        for n, (src, dst) in enumerate(
            [(trow_hbm, trow), (tcnt_hbm, tcnt), (own_hbm, own), (spl_hbm, spl), (mode_hbm, mode)]
        )
    ]

    def kern_copy(p):
        at = pl.ds(2 * p, 2)
        return pltpu.make_async_copy(kern_hbm.at[at], kern.at[at], kern_sem.at[p])

    for p in range(pairs):
        kern_copy(p).start()
    for copy in small:
        copy.start()

    hist_copy.wait()
    cuts = [0, 2 * BLOCK, 4 * BLOCK, 6 * BLOCK, hlen]
    hist_sends = []
    for n in range(4):
        lo, size = cuts[n], cuts[n + 1] - cuts[n]
        hist_t[lo : lo + size, :] = hist_in[:, lo : lo + size].T
        if n == 0:
            pl.semaphore_wait(barrier, rows)
        send = pltpu.make_async_remote_copy(
            src_ref=hist_t.at[pl.ds(lo, size)],
            dst_ref=window.at[pl.ds(pl.multiple_of(half * lag + lo, half), size)],
            send_sem=hist_sem.at[n],
            recv_sem=hist_sem.at[4 + n],
            device_id={"lag": 1 - lag},
            device_id_type=MESH_ID,
        )
        send.start()
        hist_sends.append(send)
    window[pl.ds(pl.multiple_of(hlen * lag, half), half), :] = hist_t[
        pl.ds(pl.multiple_of((hlen - half) * (1 - lag), half), half), :
    ]

    for copy in small:
        copy.wait()
    tiles, tp = trow.shape
    picks = tiles * tp
    e_lane = lax.broadcasted_iota(jnp.int32, (tp, picks), 1)
    e_row = lax.broadcasted_iota(jnp.int32, (tp, picks), 0)
    spread = (lax.rem(e_lane, tp) == e_row).astype(BF16)
    t_lane = lax.broadcasted_iota(jnp.int32, (tiles, picks), 1)
    t_row = lax.broadcasted_iota(jnp.int32, (tiles, picks), 0)
    mine = lax.div(t_lane, tp) == t_row
    row_at = jnp.dot(trow[...].astype(F32).astype(BF16), spread, preferred_element_type=F32)
    row_at = jnp.sum(jnp.where(mine, row_at, 0.0), axis=0, keepdims=True)
    lane = lax.broadcasted_iota(jnp.int32, (1, picks), 1)
    tile_at = lax.div(lane, tp)
    count_at = jnp.zeros((1, picks), jnp.int32)
    own_at = jnp.zeros((1, picks), jnp.int32)
    for i in range(tiles):
        count_at = jnp.where(tile_at == i, tcnt[i], count_at)
        own_at = jnp.where(tile_at == i, own[i], own_at)
    row_at = jnp.where(lax.rem(lane, tp) < count_at, row_at, -1.0)
    r_iota = lax.broadcasted_iota(jnp.int32, (BLOCK, picks), 0).astype(F32)
    picker = (r_iota == row_at).astype(F32).astype(BF16)

    modes_t = mode[...].T
    mode_hi = modes_t.astype(BF16)
    mode_lo = (modes_t - mode_hi.astype(F32)).astype(BF16)
    ndof = modes_t.shape[0]
    mode_split[0:ndof, :] = mode_hi
    mode_split[ndof : 2 * ndof, :] = mode_lo
    mode_split[2 * ndof : 3 * ndof, :] = mode_hi

    for p in range(pairs):
        kern_copy(p).wait()
    for send in hist_sends:
        send.wait()

    b_lane = lax.broadcasted_iota(jnp.int32, (1, 2 * BLOCK), 1)
    shift = (BLOCK - 1) - lax.rem(b_lane, BLOCK)
    lane1 = lax.broadcasted_iota(jnp.int32, (TSTEP, BLOCK), 1)

    def pair(p, acc):
        total = None
        for a in range(blocks):
            cols = slice(a * BLOCK, (a + 1) * BLOCK)
            w = jnp.concatenate([kern[2 * p, :, cols], kern[2 * p + 1, :, cols]], axis=1)
            start = lags - BLOCK * (a + 1)
            x = window[start : start + BLOCK + TSTEP, :]
            y = jnp.dot(x, w, preferred_element_type=F32)
            total = y if total is None else total + y
        bit, length = BLOCK // 2, BLOCK
        while bit >= 8:
            length = TSTEP + bit
            up = total[bit : bit + length]
            total = jnp.where((shift & bit) != 0, up, total[:length])
            bit //= 2
        for bit in (4, 2, 1):
            up = pltpu.roll(total, total.shape[0] - bit, 0)
            total = jnp.where((shift & bit) != 0, up, total)
        total = total[:TSTEP]
        s0 = jnp.sum(total[:, :BLOCK], axis=1, keepdims=True)
        s1 = jnp.sum(total[:, BLOCK:], axis=1, keepdims=True)
        acc = jnp.where(lane1 == 2 * p, s0, acc)
        return jnp.where(lane1 == 2 * p + 1, s1, acc)

    acc = lax.fori_loop(0, pairs, pair, jnp.zeros((TSTEP, BLOCK), F32), unroll=2)
    part[...] = acc.reshape(2, half, BLOCK)
    part_send = pltpu.make_async_remote_copy(
        src_ref=part.at[1 - lag],
        dst_ref=part_in,
        send_sem=part_sem.at[0],
        recv_sem=part_sem.at[1],
        device_id={"lag": 1 - lag},
        device_id_type=MESH_ID,
    )
    part_send.start()
    part_send.wait_recv()
    pressure = (part[lag] + part_in[...]).astype(BF16)

    tile_in = jnp.dot(pressure, picker, preferred_element_type=F32)
    owned = jnp.concatenate(
        [jnp.where(own_at == d, tile_in, 0.0) for d in range(rows)], axis=0
    ).astype(BF16)
    flat = jnp.dot(owned, spl[...].reshape(picks, spl.shape[2]), preferred_element_type=F32)
    force[...] = flat.reshape(rows, half, spl.shape[2])

    def exchange(sources, dest, ssem, rsem):
        copies = [
            pltpu.make_async_remote_copy(
                src_ref=sources(lax.rem(me + o, rows)),
                dst_ref=dest.at[o - 1],
                send_sem=ssem.at[o - 1],
                recv_sem=rsem.at[o - 1],
                device_id={"row": lax.rem(me + o, rows)},
                device_id_type=MESH_ID,
            )
            for o in range(1, rows)
        ]
        for copy in copies:
            copy.start()
        return copies

    force_copies = exchange(lambda d: force.at[d], force_in, force_ssem, force_rsem)
    nodal = force[me]
    for o, copy in enumerate(force_copies):
        copy.wait_recv()
        nodal = nodal + force_in[o].astype(F32)
    nodal_hi = nodal.astype(BF16)
    nodal_lo = (nodal - nodal_hi.astype(F32)).astype(BF16)
    share = jnp.dot(
        jnp.concatenate([nodal_hi, nodal_hi, nodal_lo], axis=1),
        mode_split[...],
        preferred_element_type=F32,
    )
    modal_send[...] = share.astype(modal_send.dtype)
    modal_copies = exchange(lambda d: modal_send, modal_in, modal_ssem, modal_rsem)
    nodal_out[...] = nodal
    for o, copy in enumerate(modal_copies):
        copy.wait_recv()
        share = share + modal_in[o].astype(F32)
    modal_out[...] = share
    part_send.wait_send()
    for copy in force_copies + modal_copies:
        copy.wait_send()


def on_device(history, kernel, tile_rows, tile_counts, owner, spline, mode_shapes):
    rows = lax.axis_size("row")
    modes, hlen = history.shape
    press, _, lags = kernel.shape
    tiles, tp = tile_rows.shape
    ndof = spline.shape[2]
    half = TSTEP // 2
    dma = pltpu.SemaphoreType.DMA
    return pl.pallas_call(
        functools.partial(body, rows),
        out_shape=(
            pltpu.VMEM((half, ndof), F32),
            pltpu.VMEM((half, modes), F32),
        ),
        in_specs=[pl.BlockSpec(memory_space=pltpu.HBM)] * 7,
        out_specs=(
            pl.BlockSpec(memory_space=pltpu.VMEM),
            pl.BlockSpec(memory_space=pltpu.VMEM),
        ),
        scratch_shapes=[
            pltpu.VMEM((modes, hlen), BF16),
            pltpu.VMEM((press, modes, lags), BF16),
            pltpu.VMEM((tiles, tp), jnp.int32),
            pltpu.SMEM((tiles,), jnp.int32),
            pltpu.SMEM((tiles,), jnp.int32),
            pltpu.VMEM(spline.shape, BF16),
            pltpu.VMEM((modes, ndof), F32),
            pltpu.VMEM((3 * ndof, modes), BF16),
            pltpu.VMEM((hlen, modes), BF16),
            pltpu.VMEM((hlen + half, modes), BF16),
            pltpu.VMEM((2, half, BLOCK), F32),
            pltpu.VMEM((half, BLOCK), F32),
            pltpu.VMEM((rows, half, ndof), F32),
            pltpu.VMEM((rows - 1, half, ndof), F32),
            pltpu.VMEM((half, modes), BF16),
            pltpu.VMEM((rows - 1, half, modes), BF16),
            dma((6,)),
            dma((press // 2,)),
            dma((8,)),
            dma((2,)),
            dma((rows - 1,)),
            dma((rows - 1,)),
            dma((rows - 1,)),
            dma((rows - 1,)),
        ],
        compiler_params=pltpu.CompilerParams(
            collective_id=0, has_side_effects=True, vmem_limit_bytes=61440 * 1024
        ),
    )(history, kernel, tile_rows, tile_counts, owner.reshape(tiles), spline, mode_shapes.T)


def solution(mesh):
    return jax.shard_map(
        on_device,
        mesh=mesh,
        in_specs=(
            P("grp", "lag"),
            P(("grp", "row"), None, "lag"),
            P(("grp", "row"), None),
            P(("grp", "row")),
            P(("grp", "row"), None),
            P(("grp", "row"), None, None),
            P(("grp", "row"), None),
        ),
        out_specs=(P("lag", ("grp", "row")), P("lag", "grp")),
        check_vma=False,
    )
```

```python
import functools

import jax
import jax.numpy as jnp
from jax import lax
from jax.experimental import pallas as pl
from jax.experimental.pallas import tpu as pltpu
from jax.sharding import PartitionSpec as P

TSTEP = 32
BLOCK = 128
MESH_ID = pl.DeviceIdType.MESH
F32 = jnp.float32
BF16 = jnp.bfloat16


def body(
    rows,
    hist_hbm,
    kern_hbm,
    trow_hbm,
    tcnt_hbm,
    own_hbm,
    spl_hbm,
    mode_hbm,
    nodal_out,
    modal_out,
    hist_in,
    kern,
    trow,
    tcnt,
    own,
    spl,
    mode,
    mode_split,
    hist_t,
    window,
    part,
    part_in,
    force,
    force_in,
    modal_send,
    modal_in,
    local_sem,
    kern_sem,
    hist_sem,
    part_sem,
    force_ssem,
    force_rsem,
    modal_ssem,
    modal_rsem,
):
    lag = lax.axis_index("lag")
    me = lax.axis_index("row")
    press = kern.shape[0]
    pairs = press // 2
    lags = kern.shape[2]
    blocks = lags // BLOCK
    hlen = hist_in.shape[1]
    half = TSTEP // 2

    cuts = [0, 2 * BLOCK, 4 * BLOCK, 6 * BLOCK, hlen]
    spans = [(cuts[n], cuts[n + 1] - cuts[n]) for n in range(4)]
    hist_copies = [
        pltpu.make_async_copy(
            hist_hbm.at[:, pl.ds(lo, size)], hist_in.at[:, pl.ds(lo, size)], local_sem.at[6 + n]
        )
        for n, (lo, size) in enumerate(spans)
    ]
    for copy in hist_copies:
        copy.start()
    barrier = pltpu.get_barrier_semaphore()
    pl.semaphore_signal(barrier, inc=1, device_id={"lag": 1 - lag}, device_id_type=MESH_ID)
    for o in range(1, rows):
        pl.semaphore_signal(
            barrier, inc=1, device_id={"row": lax.rem(me + o, rows)}, device_id_type=MESH_ID
        )
    small = [
        pltpu.make_async_copy(src, dst, local_sem.at[1 + n])
        for n, (src, dst) in enumerate(
            [(trow_hbm, trow), (tcnt_hbm, tcnt), (own_hbm, own), (spl_hbm, spl), (mode_hbm, mode)]
        )
    ]

    def kern_copy(p):
        at = pl.ds(2 * p, 2)
        return pltpu.make_async_copy(kern_hbm.at[at], kern.at[at], kern_sem.at[p])

    for p in range(pairs):
        kern_copy(p).start()
    for copy in small:
        copy.start()

    hist_sends = []
    for n, (lo, size) in enumerate(spans):
        hist_copies[n].wait()
        hist_t[lo : lo + size, :] = hist_in[:, lo : lo + size].T
        if n == 0:
            pl.semaphore_wait(barrier, rows)
        send = pltpu.make_async_remote_copy(
            src_ref=hist_t.at[pl.ds(lo, size)],
            dst_ref=window.at[pl.ds(pl.multiple_of(half * lag + lo, half), size)],
            send_sem=hist_sem.at[n],
            recv_sem=hist_sem.at[4 + n],
            device_id={"lag": 1 - lag},
            device_id_type=MESH_ID,
        )
        send.start()
        hist_sends.append(send)
    window[pl.ds(pl.multiple_of(hlen * lag, half), half), :] = hist_t[
        pl.ds(pl.multiple_of((hlen - half) * (1 - lag), half), half), :
    ]

    for copy in small:
        copy.wait()
    tiles, tp = trow.shape
    picks = tiles * tp
    e_lane = lax.broadcasted_iota(jnp.int32, (tp, picks), 1)
    e_row = lax.broadcasted_iota(jnp.int32, (tp, picks), 0)
    spread = (lax.rem(e_lane, tp) == e_row).astype(BF16)
    t_lane = lax.broadcasted_iota(jnp.int32, (tiles, picks), 1)
    t_row = lax.broadcasted_iota(jnp.int32, (tiles, picks), 0)
    mine = lax.div(t_lane, tp) == t_row
    row_at = jnp.dot(trow[...].astype(F32).astype(BF16), spread, preferred_element_type=F32)
    row_at = jnp.sum(jnp.where(mine, row_at, 0.0), axis=0, keepdims=True)
    lane = lax.broadcasted_iota(jnp.int32, (1, picks), 1)
    tile_at = lax.div(lane, tp)
    count_at = jnp.zeros((1, picks), jnp.int32)
    own_at = jnp.zeros((1, picks), jnp.int32)
    for i in range(tiles):
        count_at = jnp.where(tile_at == i, tcnt[i], count_at)
        own_at = jnp.where(tile_at == i, own[i], own_at)
    row_at = jnp.where(lax.rem(lane, tp) < count_at, row_at, -1.0)
    r_iota = lax.broadcasted_iota(jnp.int32, (BLOCK, picks), 0).astype(F32)
    picker = (r_iota == row_at).astype(F32).astype(BF16)

    modes_t = mode[...].T
    mode_hi = modes_t.astype(BF16)
    mode_lo = (modes_t - mode_hi.astype(F32)).astype(BF16)
    ndof = modes_t.shape[0]
    mode_split[0:ndof, :] = mode_hi
    mode_split[ndof : 2 * ndof, :] = mode_lo
    mode_split[2 * ndof : 3 * ndof, :] = mode_hi

    for p in range(pairs):
        kern_copy(p).wait()
    for send in hist_sends:
        send.wait()

    b_lane = lax.broadcasted_iota(jnp.int32, (1, 2 * BLOCK), 1)
    shift = (BLOCK - 1) - lax.rem(b_lane, BLOCK)
    lane1 = lax.broadcasted_iota(jnp.int32, (TSTEP, BLOCK), 1)

    def pair(p, acc):
        total = None
        for a in range(blocks):
            cols = slice(a * BLOCK, (a + 1) * BLOCK)
            w = jnp.concatenate([kern[2 * p, :, cols], kern[2 * p + 1, :, cols]], axis=1)
            start = lags - BLOCK * (a + 1)
            x = window[start : start + BLOCK + TSTEP, :]
            y = jnp.dot(x, w, preferred_element_type=F32)
            total = y if total is None else total + y
        bit, length = BLOCK // 2, BLOCK
        while bit >= 8:
            length = TSTEP + bit
            up = total[bit : bit + length]
            total = jnp.where((shift & bit) != 0, up, total[:length])
            bit //= 2
        for bit in (4, 2, 1):
            up = pltpu.roll(total, total.shape[0] - bit, 0)
            total = jnp.where((shift & bit) != 0, up, total)
        total = total[:TSTEP]
        s0 = jnp.sum(total[:, :BLOCK], axis=1, keepdims=True)
        s1 = jnp.sum(total[:, BLOCK:], axis=1, keepdims=True)
        acc = jnp.where(lane1 == 2 * p, s0, acc)
        return jnp.where(lane1 == 2 * p + 1, s1, acc)

    acc = lax.fori_loop(0, pairs, pair, jnp.zeros((TSTEP, BLOCK), F32), unroll=4)
    part[...] = acc.reshape(2, half, BLOCK)
    part_send = pltpu.make_async_remote_copy(
        src_ref=part.at[1 - lag],
        dst_ref=part_in,
        send_sem=part_sem.at[0],
        recv_sem=part_sem.at[1],
        device_id={"lag": 1 - lag},
        device_id_type=MESH_ID,
    )
    part_send.start()
    part_send.wait_recv()
    pressure = (part[lag] + part_in[...]).astype(BF16)

    tile_in = jnp.dot(pressure, picker, preferred_element_type=F32)
    owned = jnp.concatenate(
        [jnp.where(own_at == d, tile_in, 0.0) for d in range(rows)], axis=0
    ).astype(BF16)
    flat = jnp.dot(owned, spl[...].reshape(picks, spl.shape[2]), preferred_element_type=F32)
    force[...] = flat.reshape(rows, half, spl.shape[2])

    def exchange(sources, dest, ssem, rsem):
        copies = [
            pltpu.make_async_remote_copy(
                src_ref=sources(lax.rem(me + o, rows)),
                dst_ref=dest.at[o - 1],
                send_sem=ssem.at[o - 1],
                recv_sem=rsem.at[o - 1],
                device_id={"row": lax.rem(me + o, rows)},
                device_id_type=MESH_ID,
            )
            for o in range(1, rows)
        ]
        for copy in copies:
            copy.start()
        return copies

    force_copies = exchange(lambda d: force.at[d], force_in, force_ssem, force_rsem)
    nodal = force[me]
    for o, copy in enumerate(force_copies):
        copy.wait_recv()
        nodal = nodal + force_in[o].astype(F32)
    nodal_hi = nodal.astype(BF16)
    nodal_lo = (nodal - nodal_hi.astype(F32)).astype(BF16)
    share = jnp.dot(
        jnp.concatenate([nodal_hi, nodal_hi, nodal_lo], axis=1),
        mode_split[...],
        preferred_element_type=F32,
    )
    modal_send[...] = share.astype(modal_send.dtype)
    modal_copies = exchange(lambda d: modal_send, modal_in, modal_ssem, modal_rsem)
    nodal_out[...] = nodal
    for o, copy in enumerate(modal_copies):
        copy.wait_recv()
        share = share + modal_in[o].astype(F32)
    modal_out[...] = share
    part_send.wait_send()
    for copy in force_copies + modal_copies:
        copy.wait_send()


def write_out(nodal, modal, nodal_out, modal_out, sem):
    copies = [
        pltpu.make_async_copy(nodal, nodal_out, sem.at[0]),
        pltpu.make_async_copy(modal, modal_out, sem.at[1]),
    ]
    for copy in copies:
        copy.start()
    for copy in copies:
        copy.wait()


def on_device(history, kernel, tile_rows, tile_counts, owner, spline, mode_shapes):
    rows = lax.axis_size("row")
    modes, hlen = history.shape
    press, _, lags = kernel.shape
    tiles, tp = tile_rows.shape
    ndof = spline.shape[2]
    half = TSTEP // 2
    dma = pltpu.SemaphoreType.DMA
    nodal, modal = pl.pallas_call(
        functools.partial(body, rows),
        out_shape=(
            pltpu.VMEM((half, ndof), F32),
            pltpu.VMEM((half, modes), F32),
        ),
        in_specs=[pl.BlockSpec(memory_space=pltpu.HBM)] * 7,
        out_specs=(
            pl.BlockSpec(memory_space=pltpu.VMEM),
            pl.BlockSpec(memory_space=pltpu.VMEM),
        ),
        scratch_shapes=[
            pltpu.VMEM((modes, hlen), BF16),
            pltpu.VMEM((press, modes, lags), BF16),
            pltpu.VMEM((tiles, tp), jnp.int32),
            pltpu.SMEM((tiles,), jnp.int32),
            pltpu.SMEM((tiles,), jnp.int32),
            pltpu.VMEM(spline.shape, BF16),
            pltpu.VMEM((modes, ndof), F32),
            pltpu.VMEM((3 * ndof, modes), BF16),
            pltpu.VMEM((hlen, modes), BF16),
            pltpu.VMEM((hlen + half, modes), BF16),
            pltpu.VMEM((2, half, BLOCK), F32),
            pltpu.VMEM((half, BLOCK), F32),
            pltpu.VMEM((rows, half, ndof), F32),
            pltpu.VMEM((rows - 1, half, ndof), F32),
            pltpu.VMEM((half, modes), BF16),
            pltpu.VMEM((rows - 1, half, modes), BF16),
            dma((10,)),
            dma((press // 2,)),
            dma((8,)),
            dma((2,)),
            dma((rows - 1,)),
            dma((rows - 1,)),
            dma((rows - 1,)),
            dma((rows - 1,)),
        ],
        compiler_params=pltpu.CompilerParams(
            collective_id=0, has_side_effects=True, vmem_limit_bytes=61440 * 1024
        ),
    )(history, kernel, tile_rows, tile_counts, owner.reshape(tiles), spline, mode_shapes.T)
    return pl.pallas_call(
        write_out,
        out_shape=(pltpu.HBM((half, ndof), F32), pltpu.HBM((half, modes), F32)),
        in_specs=[pl.BlockSpec(memory_space=pltpu.VMEM)] * 2,
        out_specs=(pl.BlockSpec(memory_space=pltpu.HBM), pl.BlockSpec(memory_space=pltpu.HBM)),
        scratch_shapes=[dma((2,))],
        compiler_params=pltpu.CompilerParams(vmem_limit_bytes=1024 * 1024),
    )(nodal, modal)


def solution(mesh):
    return jax.shard_map(
        on_device,
        mesh=mesh,
        in_specs=(
            P("grp", "lag"),
            P(("grp", "row"), None, "lag"),
            P(("grp", "row"), None),
            P(("grp", "row")),
            P(("grp", "row"), None),
            P(("grp", "row"), None, None),
            P(("grp", "row"), None),
        ),
        out_specs=(P("lag", ("grp", "row")), P("lag", "grp")),
        check_vma=False,
    )
```

```python
import functools

import jax
import jax.numpy as jnp
from jax import lax
from jax.experimental import pallas as pl
from jax.experimental.pallas import tpu as pltpu
from jax.sharding import PartitionSpec as P

TSTEP = 32
BLOCK = 128
MESH_ID = pl.DeviceIdType.MESH
F32 = jnp.float32
BF16 = jnp.bfloat16


def body(
    rows,
    hist_hbm,
    kern_hbm,
    trow_hbm,
    tcnt_hbm,
    own_hbm,
    spl_hbm,
    mode_hbm,
    nodal_out,
    modal_out,
    hist_in,
    kern,
    trow,
    tcnt,
    own,
    spl,
    mode,
    mode_split,
    hist_t,
    window,
    part,
    part_in,
    force,
    force_in,
    modal_send,
    modal_in,
    local_sem,
    kern_sem,
    hist_sem,
    part_sem,
    force_ssem,
    force_rsem,
    modal_ssem,
    modal_rsem,
):
    lag = lax.axis_index("lag")
    me = lax.axis_index("row")
    press = kern.shape[0]
    pairs = press // 2
    lags = kern.shape[2]
    blocks = lags // BLOCK
    hlen = hist_in.shape[1]
    half = TSTEP // 2

    cuts = [0, 2 * BLOCK, 4 * BLOCK, 6 * BLOCK, hlen]
    spans = [(cuts[n], cuts[n + 1] - cuts[n]) for n in range(4)]
    hist_copies = [
        pltpu.make_async_copy(
            hist_hbm.at[:, pl.ds(lo, size)], hist_in.at[:, pl.ds(lo, size)], local_sem.at[6 + n]
        )
        for n, (lo, size) in enumerate(spans)
    ]
    for copy in hist_copies:
        copy.start()
    barrier = pltpu.get_barrier_semaphore()
    pl.semaphore_signal(barrier, inc=1, device_id={"lag": 1 - lag}, device_id_type=MESH_ID)
    for o in range(1, rows):
        pl.semaphore_signal(
            barrier, inc=1, device_id={"row": lax.rem(me + o, rows)}, device_id_type=MESH_ID
        )
    small = [
        pltpu.make_async_copy(src, dst, local_sem.at[1 + n])
        for n, (src, dst) in enumerate(
            [(trow_hbm, trow), (tcnt_hbm, tcnt), (own_hbm, own), (spl_hbm, spl), (mode_hbm, mode)]
        )
    ]

    def kern_copy(p):
        at = pl.ds(2 * p, 2)
        return pltpu.make_async_copy(kern_hbm.at[at], kern.at[at], kern_sem.at[p])

    for p in range(pairs):
        kern_copy(p).start()
    for copy in small:
        copy.start()

    hist_sends = []
    for n, (lo, size) in enumerate(spans):
        hist_copies[n].wait()
        hist_t[lo : lo + size, :] = hist_in[:, lo : lo + size].T
        if n == 0:
            pl.semaphore_wait(barrier, rows)
        send = pltpu.make_async_remote_copy(
            src_ref=hist_t.at[pl.ds(lo, size)],
            dst_ref=window.at[pl.ds(pl.multiple_of(half * lag + lo, half), size)],
            send_sem=hist_sem.at[n],
            recv_sem=hist_sem.at[4 + n],
            device_id={"lag": 1 - lag},
            device_id_type=MESH_ID,
        )
        send.start()
        hist_sends.append(send)
    window[pl.ds(pl.multiple_of(hlen * lag, half), half), :] = hist_t[
        pl.ds(pl.multiple_of((hlen - half) * (1 - lag), half), half), :
    ]

    for copy in small:
        copy.wait()
    tiles, tp = trow.shape
    picks = tiles * tp
    e_lane = lax.broadcasted_iota(jnp.int32, (tp, picks), 1)
    e_row = lax.broadcasted_iota(jnp.int32, (tp, picks), 0)
    spread = (lax.rem(e_lane, tp) == e_row).astype(BF16)
    t_lane = lax.broadcasted_iota(jnp.int32, (tiles, picks), 1)
    t_row = lax.broadcasted_iota(jnp.int32, (tiles, picks), 0)
    mine = lax.div(t_lane, tp) == t_row
    row_at = jnp.dot(trow[...].astype(F32).astype(BF16), spread, preferred_element_type=F32)
    row_at = jnp.sum(jnp.where(mine, row_at, 0.0), axis=0, keepdims=True)
    lane = lax.broadcasted_iota(jnp.int32, (1, picks), 1)
    tile_at = lax.div(lane, tp)
    count_at = jnp.zeros((1, picks), jnp.int32)
    own_at = jnp.zeros((1, picks), jnp.int32)
    for i in range(tiles):
        count_at = jnp.where(tile_at == i, tcnt[i], count_at)
        own_at = jnp.where(tile_at == i, own[i], own_at)
    row_at = jnp.where(lax.rem(lane, tp) < count_at, row_at, -1.0)
    r_iota = lax.broadcasted_iota(jnp.int32, (BLOCK, picks), 0).astype(F32)
    picker = (r_iota == row_at).astype(F32).astype(BF16)

    modes_t = mode[...].T
    mode_hi = modes_t.astype(BF16)
    mode_lo = (modes_t - mode_hi.astype(F32)).astype(BF16)
    ndof = modes_t.shape[0]
    mode_split[0:ndof, :] = mode_hi
    mode_split[ndof : 2 * ndof, :] = mode_lo
    mode_split[2 * ndof : 3 * ndof, :] = mode_hi

    for p in range(pairs):
        kern_copy(p).wait()
    for send in hist_sends:
        send.wait()

    b_lane = lax.broadcasted_iota(jnp.int32, (1, 2 * BLOCK), 1)
    shift = (BLOCK - 1) - lax.rem(b_lane, BLOCK)
    lane1 = lax.broadcasted_iota(jnp.int32, (TSTEP, BLOCK), 1)

    def pair(p, acc):
        total = None
        for a in range(blocks):
            cols = slice(a * BLOCK, (a + 1) * BLOCK)
            w = jnp.concatenate([kern[2 * p, :, cols], kern[2 * p + 1, :, cols]], axis=1)
            start = lags - BLOCK * (a + 1)
            x = window[start : start + BLOCK + TSTEP, :]
            y = jnp.dot(x, w, preferred_element_type=F32)
            total = y if total is None else total + y
        bit, length = BLOCK // 2, BLOCK
        while bit >= 8:
            length = TSTEP + bit
            up = total[bit : bit + length]
            total = jnp.where((shift & bit) != 0, up, total[:length])
            bit //= 2
        for bit in (4, 2, 1):
            up = pltpu.roll(total, total.shape[0] - bit, 0)
            total = jnp.where((shift & bit) != 0, up, total)
        total = total[:TSTEP]
        s0 = jnp.sum(total[:, :BLOCK], axis=1, keepdims=True)
        s1 = jnp.sum(total[:, BLOCK:], axis=1, keepdims=True)
        acc = jnp.where(lane1 == 2 * p, s0, acc)
        return jnp.where(lane1 == 2 * p + 1, s1, acc)

    acc = lax.fori_loop(0, pairs, pair, jnp.zeros((TSTEP, BLOCK), F32), unroll=8)
    part[...] = acc.reshape(2, half, BLOCK)
    part_send = pltpu.make_async_remote_copy(
        src_ref=part.at[1 - lag],
        dst_ref=part_in,
        send_sem=part_sem.at[0],
        recv_sem=part_sem.at[1],
        device_id={"lag": 1 - lag},
        device_id_type=MESH_ID,
    )
    part_send.start()
    part_send.wait_recv()
    pressure = (part[lag] + part_in[...]).astype(BF16)

    tile_in = jnp.dot(pressure, picker, preferred_element_type=F32)
    owned = jnp.concatenate(
        [jnp.where(own_at == d, tile_in, 0.0) for d in range(rows)], axis=0
    ).astype(BF16)
    flat = jnp.dot(owned, spl[...].reshape(picks, spl.shape[2]), preferred_element_type=F32)
    force[...] = flat.reshape(rows, half, spl.shape[2])

    def exchange(sources, dest, ssem, rsem):
        copies = [
            pltpu.make_async_remote_copy(
                src_ref=sources(lax.rem(me + o, rows)),
                dst_ref=dest.at[o - 1],
                send_sem=ssem.at[o - 1],
                recv_sem=rsem.at[o - 1],
                device_id={"row": lax.rem(me + o, rows)},
                device_id_type=MESH_ID,
            )
            for o in range(1, rows)
        ]
        for copy in copies:
            copy.start()
        return copies

    force_copies = exchange(lambda d: force.at[d], force_in, force_ssem, force_rsem)
    nodal = force[me]
    for o, copy in enumerate(force_copies):
        copy.wait_recv()
        nodal = nodal + force_in[o].astype(F32)
    nodal_hi = nodal.astype(BF16)
    nodal_lo = (nodal - nodal_hi.astype(F32)).astype(BF16)
    share = jnp.dot(
        jnp.concatenate([nodal_hi, nodal_hi, nodal_lo], axis=1),
        mode_split[...],
        preferred_element_type=F32,
    )
    modal_send[...] = share.astype(modal_send.dtype)
    modal_copies = exchange(lambda d: modal_send, modal_in, modal_ssem, modal_rsem)
    nodal_out[...] = nodal
    for o, copy in enumerate(modal_copies):
        copy.wait_recv()
        share = share + modal_in[o].astype(F32)
    modal_out[...] = share
    part_send.wait_send()
    for copy in force_copies + modal_copies:
        copy.wait_send()


def write_out(nodal, modal, nodal_out, modal_out, sem):
    copies = [
        pltpu.make_async_copy(nodal, nodal_out, sem.at[0]),
        pltpu.make_async_copy(modal, modal_out, sem.at[1]),
    ]
    for copy in copies:
        copy.start()
    for copy in copies:
        copy.wait()


def on_device(history, kernel, tile_rows, tile_counts, owner, spline, mode_shapes):
    rows = lax.axis_size("row")
    modes, hlen = history.shape
    press, _, lags = kernel.shape
    tiles, tp = tile_rows.shape
    ndof = spline.shape[2]
    half = TSTEP // 2
    dma = pltpu.SemaphoreType.DMA
    nodal, modal = pl.pallas_call(
        functools.partial(body, rows),
        out_shape=(
            pltpu.VMEM((half, ndof), F32),
            pltpu.VMEM((half, modes), F32),
        ),
        in_specs=[pl.BlockSpec(memory_space=pltpu.HBM)] * 7,
        out_specs=(
            pl.BlockSpec(memory_space=pltpu.VMEM),
            pl.BlockSpec(memory_space=pltpu.VMEM),
        ),
        scratch_shapes=[
            pltpu.VMEM((modes, hlen), BF16),
            pltpu.VMEM((press, modes, lags), BF16),
            pltpu.VMEM((tiles, tp), jnp.int32),
            pltpu.SMEM((tiles,), jnp.int32),
            pltpu.SMEM((tiles,), jnp.int32),
            pltpu.VMEM(spline.shape, BF16),
            pltpu.VMEM((modes, ndof), F32),
            pltpu.VMEM((3 * ndof, modes), BF16),
            pltpu.VMEM((hlen, modes), BF16),
            pltpu.VMEM((hlen + half, modes), BF16),
            pltpu.VMEM((2, half, BLOCK), F32),
            pltpu.VMEM((half, BLOCK), F32),
            pltpu.VMEM((rows, half, ndof), F32),
            pltpu.VMEM((rows - 1, half, ndof), F32),
            pltpu.VMEM((half, modes), BF16),
            pltpu.VMEM((rows - 1, half, modes), BF16),
            dma((10,)),
            dma((press // 2,)),
            dma((8,)),
            dma((2,)),
            dma((rows - 1,)),
            dma((rows - 1,)),
            dma((rows - 1,)),
            dma((rows - 1,)),
        ],
        compiler_params=pltpu.CompilerParams(
            collective_id=0, has_side_effects=True, vmem_limit_bytes=61440 * 1024
        ),
    )(history, kernel, tile_rows, tile_counts, owner.reshape(tiles), spline, mode_shapes.T)
    return pl.pallas_call(
        write_out,
        out_shape=(pltpu.HBM((half, ndof), F32), pltpu.HBM((half, modes), F32)),
        in_specs=[pl.BlockSpec(memory_space=pltpu.VMEM)] * 2,
        out_specs=(pl.BlockSpec(memory_space=pltpu.HBM), pl.BlockSpec(memory_space=pltpu.HBM)),
        scratch_shapes=[dma((2,))],
        compiler_params=pltpu.CompilerParams(vmem_limit_bytes=1024 * 1024),
    )(nodal, modal)


def solution(mesh):
    return jax.shard_map(
        on_device,
        mesh=mesh,
        in_specs=(
            P("grp", "lag"),
            P(("grp", "row"), None, "lag"),
            P(("grp", "row"), None),
            P(("grp", "row")),
            P(("grp", "row"), None),
            P(("grp", "row"), None, None),
            P(("grp", "row"), None),
        ),
        out_specs=(P("lag", ("grp", "row")), P("lag", "grp")),
        check_vma=False,
    )
```
